32 devices in a mesh: groups: 2 (over y), row: 16 (over z, x, core).
Axes of the slice: x: 2, y: 2, z: 4, core: 2. Of those that a mesh axis runs over, the one named last changes fastest.
Arguments:
- tokens: bfloat16 [64, 8192], P(('groups', 'row')), parts along dimension 0, may hold values from -6 to 6
- norm_gain: float32 [8192], replicated, may hold values from 0.1 to 1.9
- gate_weight: bfloat16 [8192, 26624], P(None, 'row'), may hold values from -0.0625 to 0.0625
- up_weight: bfloat16 [8192, 26624], P(None, 'row'), may hold values from -0.0625 to 0.0625
- down_weight: bfloat16 [26624, 8192], P('row'), may hold values from -0.0390625 to 0.0390625
Outputs:
- scored: bfloat16 [64, 8192], P(('groups', 'row')), parts along dimension 0
The draws below stay inside these ranges and needn't reach their ends.
There are 2 independent parts, one for each index of `groups`. The reference program is written for one: setup_inputs(seed, part) draws one part's arguments, and reference() takes and returns one part's arrays. A program takes and returns all parts, laid end to end along the dimension named above; an argument that names none is the same for every part. Nothing has to cross between parts.
All inputs are finite; a program needn't handle non-finite values.
Results may differ from the reference program's by a relative error of at most 0.0065.
Values may be sent and summed in bfloat16 or wider, within the bound.
A program may use at most 192 MiB of HBM per device.

```python
import jax
import jax.numpy as jnp
from jax import lax

D = 8192
FF = 26624
TOKENS = 32


def block_scale(own_key, extent, pieces, smallest, largest):
    loudness, own = 1.0, jax.random.fold_in(own_key, 6)
    for position, shards_of in pieces:
        heights = jnp.exp(jax.random.uniform(jax.random.fold_in(own, position), (shards_of,), jnp.float32, smallest / len(pieces), largest / len(pieces)))
        loudness = loudness * jnp.repeat(heights, extent[position] // shards_of).reshape([-1 if axis == position else 1 for axis in range(len(extent))])
    return loudness


def scatter_about(rng, dims, scale, reach, pieces=(), kind=jnp.bfloat16):
    level = block_scale(rng, dims, pieces, -0.22, 0.18) if pieces else 1.0
    array = jax.random.normal(rng, dims, jnp.float32) * scale * level
    return jnp.minimum(jnp.maximum(array, -reach), reach).astype(kind)


def setup_inputs(seed: int = 0, part: int = 0) -> dict:
    keys = jax.random.split(jax.random.key(seed), 6)
    part_keys = jax.random.split(jax.random.fold_in(keys[5], part), 6)
    return {
        "tokens": scatter_about(part_keys[0], (TOKENS, D), 1.0, 6.0, ((0, 16),)),
        "norm_gain": jnp.clip(1.0 + 0.18 * jax.random.normal(keys[1], (D,), jnp.float32), 0.1, 1.9),
        "gate_weight": scatter_about(keys[2], (D, FF), D ** -0.5, 0.0625, ((1, 16),)),
        "up_weight": scatter_about(keys[3], (D, FF), D ** -0.5, 0.0625, ((1, 16),)),
        "down_weight": scatter_about(keys[4], (FF, D), FF ** -0.5, 0.0390625, ((0, 16),)),
    }


epsilon = 1e-05

def normalize(tokens, norm_gain):
    floated = tokens.astype(jnp.float32)
    mean_square = lax.optimization_barrier(jnp.mean(floated * floated, axis=-1, keepdims=True))
    return (floated * jax.lax.rsqrt(mean_square + epsilon) * norm_gain).astype(jnp.bfloat16)

def reference(tokens, norm_gain, gate_weight, up_weight, down_weight):
    normed = normalize(tokens, norm_gain)
    gate_out = jnp.dot(normed, gate_weight, preferred_element_type=jnp.float32)
    up_out = jnp.dot(normed, up_weight, preferred_element_type=jnp.float32)
    hidden = (jax.nn.silu(gate_out) * up_out).astype(jnp.bfloat16)
    return jnp.dot(hidden, down_weight, preferred_element_type=jnp.float32).astype(jnp.bfloat16)
```

```python
import functools

import jax
import jax.numpy as jnp
from jax import lax
from jax.experimental import pallas as pl
from jax.experimental.pallas import tpu as pltpu
from jax.sharding import PartitionSpec as P

epsilon = 1e-05
LANES = 128
K_CHUNK = 512
N_CHUNK = 1024
RING = 22
DOWN_RING = 4
MESH = pl.DeviceIdType.MESH


def whole_wait(ref, sem):
    pltpu.make_async_copy(ref, ref, sem).wait()


def kernel(
    chips,
    tokens_hbm,
    gain_hbm,
    gate_hbm,
    up_hbm,
    down_hbm,
    out_ref,
    tokens,
    gain,
    spread,
    piece,
    gathered,
    gathered_f32,
    x,
    ring,
    down_ring,
    gate_acc,
    up_acc,
    hidden,
    partial,
    mine,
    sib_send,
    sib_recv,
    chip_send,
    chip_recv,
    total,
    in_sem,
    ring_sem,
    down_sem,
    ag_send_sem,
    ag_recv_sem,
    fwd_send_sem,
    fwd_recv_sem,
    sib_send_sem,
    sib_recv_sem,
    chip_send_sem,
    chip_recv_sem,
):
    own, features = tokens.shape
    slots = ring.shape[0]
    down_slots = down_ring.shape[0]
    k_steps = features // K_CHUNK
    n_steps = features // N_CHUNK
    folds = features // LANES
    chunk_folds = N_CHUNK // LANES
    rows = 2 * chips * own
    half = chips * own * chunk_folds

    group = lax.axis_index("groups")
    me = lax.axis_index("row")
    core = lax.rem(me, 2)
    chip = me // 2
    other = 1 - core

    def at(to_chip, to_core):
        return (group, 2 * to_chip + to_core)

    def peer(step):
        return lax.rem(chip + step, chips)

    def gate_up_copy(index, hbm, step, slot):
        return pltpu.make_async_copy(
            hbm.at[pl.ds(pl.multiple_of(step * K_CHUNK, K_CHUNK), K_CHUNK)],
            ring.at[slot],
            ring_sem.at[slot],
        )

    def start_weight(index):
        step, slot = index // 2, lax.rem(index, slots)

        @pl.when(lax.rem(index, 2) == 0)
        def _():
            gate_up_copy(index, gate_hbm, step, slot).start()

        @pl.when(lax.rem(index, 2) == 1)
        def _():
            gate_up_copy(index, up_hbm, step, slot).start()

    def down_copy(step):
        slot = lax.rem(step, down_slots)
        return pltpu.make_async_copy(
            down_hbm.at[:, pl.ds(pl.multiple_of(step * N_CHUNK, N_CHUNK), N_CHUNK)],
            down_ring.at[slot],
            down_sem.at[slot],
        )

    tokens_in = pltpu.make_async_copy(tokens_hbm, tokens, in_sem.at[0])
    gain_in = pltpu.make_async_copy(gain_hbm, gain, in_sem.at[1])
    tokens_in.start()
    gain_in.start()
    barrier = pltpu.get_barrier_semaphore()

    def greet(step, carry):
        pl.semaphore_signal(barrier, inc=1, device_id=at(peer(step), core), device_id_type=MESH)
        return carry

    pl.semaphore_signal(barrier, inc=1, device_id=at(chip, other), device_id_type=MESH)
    lax.fori_loop(1, chips, greet, 0)
    for index in range(slots):
        gate_up_copy(index, (gate_hbm, up_hbm)[index % 2], index // 2, index % slots).start()

    tokens_in.wait()
    gain_in.wait()
    floated = tokens[...].astype(jnp.float32)
    mean_square = jnp.mean(floated * floated, axis=-1, keepdims=True)
    normed = floated * lax.rsqrt(mean_square + epsilon) * gain[...]
    for fold in range(folds):
        spread[pl.ds(fold, own, stride=folds), :] = normed[:, fold * LANES : (fold + 1) * LANES]
    piece[...] = spread[...].astype(jnp.bfloat16)
    gathered[core, chip] = piece[...]
    pl.semaphore_wait(barrier, chips)

    def forward(which):
        return pltpu.make_async_remote_copy(
            src_ref=gathered.at[core, which],
            dst_ref=gathered.at[core, which],
            send_sem=fwd_send_sem,
            recv_sem=fwd_recv_sem,
            device_id=at(chip, other),
            device_id_type=MESH,
        )

    def announce(step, carry):
        pltpu.make_async_remote_copy(
            src_ref=piece,
            dst_ref=gathered.at[core, chip],
            send_sem=ag_send_sem,
            recv_sem=ag_recv_sem.at[chip],
            device_id=at(peer(step), core),
            device_id_type=MESH,
        ).start()
        return carry

    lax.fori_loop(1, chips, announce, 0)
    forward(chip).start()

    def pass_on(step, carry):
        which = peer(step)
        whole_wait(gathered.at[core, which], ag_recv_sem.at[which])
        forward(which).start()
        return carry

    lax.fori_loop(1, chips, pass_on, 0)
    whole_wait(gathered.at[other], fwd_recv_sem)

    gathered_f32[...] = gathered[...].astype(jnp.float32).reshape(gathered_f32.shape)
    per_step = K_CHUNK // LANES
    for fold in range(folds):
        x[fold // per_step, :, (fold % per_step) * LANES : (fold % per_step + 1) * LANES] = gathered_f32[
            pl.ds(fold, rows, stride=folds), :
        ].astype(jnp.bfloat16)
    gate_acc[...] = jnp.zeros_like(gate_acc)
    up_acc[...] = jnp.zeros_like(up_acc)

    def refill(index):
        @pl.when(index + slots < 2 * k_steps)
        def _():
            start_weight(index + slots)

        ahead = index + slots - 2 * k_steps

        @pl.when(jnp.logical_and(ahead >= 0, ahead < down_slots))
        def _():
            down_copy(ahead).start()

    def project(step, carry):
        for part, (hbm, acc) in enumerate(((gate_hbm, gate_acc), (up_hbm, up_acc))):
            index = 2 * step + part
            slot = lax.rem(index, slots)
            gate_up_copy(index, hbm, step, slot).wait()
            acc[...] += jnp.dot(x[step], ring[slot], preferred_element_type=jnp.float32)
            refill(index)
        return carry

    lax.fori_loop(0, k_steps, project, 0)
    gate_out = gate_acc[...]
    hidden[...] = (gate_out / (1.0 + jnp.exp(-gate_out)) * up_acc[...]).astype(jnp.bfloat16)

    def sibling(step):
        return pltpu.make_async_remote_copy(
            src_ref=sib_send.at[step],
            dst_ref=sib_recv.at[step],
            send_sem=sib_send_sem.at[step],
            recv_sem=sib_recv_sem.at[step],
            device_id=at(chip, other),
            device_id_type=MESH,
        )

    def produce(step):
        slot = lax.rem(step, down_slots)
        down_copy(step).wait()
        product = jnp.dot(hidden[...], down_ring[slot], preferred_element_type=jnp.float32)
        for fold in range(chunk_folds):
            partial[pl.ds(fold, rows, stride=chunk_folds), :] = product[:, fold * LANES : (fold + 1) * LANES]
        sib_send[step] = partial[pl.ds(pl.multiple_of(other * half, half), half), :].astype(jnp.bfloat16)
        mine[step] = partial[pl.ds(pl.multiple_of(core * half, half), half), :]
        sibling(step).start()

        @pl.when(step + down_slots < n_steps)
        def _():
            down_copy(step + down_slots).start()

    def exchange(step):
        sibling(step).wait_recv()
        both = mine[step] + sib_recv[step].astype(jnp.float32)
        chip_send[step] = both.astype(jnp.bfloat16).reshape(chip_send.shape[1:])

        def send(ahead, carry):
            to = peer(ahead)
            pltpu.make_async_remote_copy(
                src_ref=chip_send.at[step, to],
                dst_ref=chip_recv.at[step, chip],
                send_sem=chip_send_sem.at[step],
                recv_sem=chip_recv_sem.at[step],
                device_id=at(to, core),
                device_id_type=MESH,
            ).start()
            return carry

        lax.fori_loop(1, chips, send, 0)
        chip_recv[step, chip] = chip_send[step, chip]

    def finish(step):
        whole_wait(chip_recv.at[step, pl.ds(0, chips - 1)], chip_recv_sem.at[step])
        total[...] = jnp.sum(chip_recv[step].astype(jnp.float32), axis=0)
        for fold in range(chunk_folds):
            out_ref[:, pl.ds(pl.multiple_of(step * N_CHUNK, N_CHUNK) + fold * LANES, LANES)] = total[
                pl.ds(fold, own, stride=chunk_folds), :
            ].astype(jnp.bfloat16)

    def score(step, carry):
        produce(step)

        @pl.when(step >= 1)
        def _():
            exchange(step - 1)

        return carry

    lax.fori_loop(0, n_steps, score, 0)
    exchange(n_steps - 1)

    def close(step, carry):
        finish(step)
        return carry

    lax.fori_loop(0, n_steps, close, 0)

    def drain(step, carry):
        sibling(step).wait_send()
        whole_wait(chip_send.at[step, pl.ds(0, chips - 1)], chip_send_sem.at[step])
        return carry

    lax.fori_loop(0, n_steps, drain, 0)
    whole_wait(gathered.at[core, pl.ds(0, chips - 1)], ag_send_sem)
    whole_wait(gathered.at[core], fwd_send_sem)


def per_device(devices, tokens, norm_gain, gate_weight, up_weight, down_weight):
    own, features = tokens.shape
    units = gate_weight.shape[1]
    chips = devices // 2
    rows = devices * own
    folds = features // LANES
    k_steps, n_steps = features // K_CHUNK, features // N_CHUNK
    chunk_folds = N_CHUNK // LANES
    half = chips * own * chunk_folds
    slots, down_slots = min(RING, 2 * k_steps), min(DOWN_RING, n_steps)
    bf16, f32 = jnp.bfloat16, jnp.float32
    dma = pltpu.SemaphoreType.DMA
    return pl.pallas_call(
        functools.partial(kernel, chips),
        out_shape=jax.ShapeDtypeStruct((own, features), bf16),
        in_specs=[pl.BlockSpec(memory_space=pl.ANY)] * 5,
        out_specs=pl.BlockSpec(memory_space=pltpu.VMEM),
        scratch_shapes=[
            pltpu.VMEM((own, features), bf16),
            pltpu.VMEM((1, features), f32),
            pltpu.VMEM((own * folds, LANES), f32),
            pltpu.VMEM((own * folds, LANES), bf16),
            pltpu.VMEM((2, chips, own * folds, LANES), bf16),
            pltpu.VMEM((rows * folds, LANES), f32),
            pltpu.VMEM((k_steps, rows, K_CHUNK), bf16),
            pltpu.VMEM((slots, K_CHUNK, units), bf16),
            pltpu.VMEM((down_slots, units, N_CHUNK), bf16),
            pltpu.VMEM((rows, units), f32),
            pltpu.VMEM((rows, units), f32),
            pltpu.VMEM((rows, units), bf16),
            pltpu.VMEM((rows * chunk_folds, LANES), f32),
            pltpu.VMEM((n_steps, half, LANES), f32),
            pltpu.VMEM((n_steps, half, LANES), bf16),
            pltpu.VMEM((n_steps, half, LANES), bf16),
            pltpu.VMEM((n_steps, chips, own * chunk_folds, LANES), bf16),
            pltpu.VMEM((n_steps, chips, own * chunk_folds, LANES), bf16),
            pltpu.VMEM((own * chunk_folds, LANES), f32),
            dma((2,)),
            dma((slots,)),
            dma((down_slots,)),
            dma,
            dma((chips,)),
            dma,
            dma,
            dma((n_steps,)),
            dma((n_steps,)),
            dma((n_steps,)),
            dma((n_steps,)),
        ],
        compiler_params=pltpu.CompilerParams(
            collective_id=0, has_side_effects=True, vmem_limit_bytes=60 * 1024 * 1024
        ),
        cost_estimate=pl.CostEstimate(
            flops=6 * rows * features * units,
            bytes_accessed=6 * features * units,
            transcendentals=rows * units,
        ),
    )(tokens, norm_gain.reshape(1, features), gate_weight, up_weight, down_weight)


def solution(mesh):
    placed = (P(("groups", "row"), None), P(), P(None, "row"), P(None, "row"), P("row", None))
    return jax.shard_map(
        functools.partial(per_device, mesh.shape["row"]),
        mesh=mesh,
        in_specs=placed,
        out_specs=P(("groups", "row"), None),
        check_vma=False,
    )
```

```python
import functools

import jax
import jax.numpy as jnp
from jax import lax
from jax.experimental import pallas as pl
from jax.experimental.pallas import tpu as pltpu
from jax.sharding import PartitionSpec as P

epsilon = 1e-05
LANES = 128
TILE = 256
K_CHUNK = 1024
N_CHUNK = 1024
RING = 6
DOWN_RING = 4
PIECES = 4
WIDE = 2
MESH = pl.DeviceIdType.MESH


def whole_wait(ref, sem):
    pltpu.make_async_copy(ref, ref, sem).wait()


def each(start, stop, body):
    if stop - start <= 8:
        for step in range(start, stop):
            body(step)
    else:
        pl.loop(start, stop)(body)


def kernel(
    chips,
    tokens_hbm,
    gain_hbm,
    gate_hbm,
    up_hbm,
    down_hbm,
    out_ref,
    tokens,
    gain,
    spread,
    piece,
    gathered,
    gathered_f32,
    x,
    ring,
    down_ring,
    acc,
    hidden,
    in_sem,
    ring_sem,
    down_sem,
    ag_send_sem,
    ag_recv_sem,
    fwd_send_sem,
    fwd_recv_sem,
    *groups,
):
    own, features = tokens.shape
    units = gate_hbm.shape[1]
    slots, parts, _, width = ring.shape
    down_slots = down_ring.shape[0]
    k_steps = features // K_CHUNK
    n_steps = features // N_CHUNK
    pieces = spread.shape[0]
    folds = features // LANES // pieces
    per_step = K_CHUNK // LANES
    rows = 2 * chips * own
    groups = [groups[first : first + 10] for first in range(0, len(groups), 10)]

    group = lax.axis_index("groups")
    me = lax.axis_index("row")
    core = lax.rem(me, 2)
    chip = me // 2
    other = 1 - core

    def at(to_chip, to_core):
        return (group, 2 * to_chip + to_core)

    def peer(step):
        return lax.rem(chip + step, chips)

    barrier = pltpu.get_barrier_semaphore()
    pl.semaphore_signal(barrier, inc=1, device_id=at(chip, other), device_id_type=MESH)
    each(
        1,
        chips,
        lambda step: pl.semaphore_signal(barrier, inc=1, device_id=at(peer(step), core), device_id_type=MESH),
    )
    tokens_in = pltpu.make_async_copy(tokens_hbm, tokens, in_sem.at[0])
    gain_in = pltpu.make_async_copy(gain_hbm, gain, in_sem.at[1])
    tokens_in.start()
    gain_in.start()

    def weight_copy(step, part):
        slot = step % slots
        if parts == 1:
            to = ring.at[slot, 0, :, pl.ds(part * units, units)]
        else:
            to = ring.at[slot, part]
        return pltpu.make_async_copy(
            (gate_hbm, up_hbm)[part].at[pl.ds(step * K_CHUNK, K_CHUNK)], to, ring_sem.at[slot, part]
        )

    def down_copy(step):
        slot = step % down_slots
        return pltpu.make_async_copy(
            down_hbm.at[:, pl.ds(step * N_CHUNK, N_CHUNK)], down_ring.at[slot], down_sem.at[slot]
        )

    for step in range(slots):
        for part in range(2):
            weight_copy(step, part).start()

    tokens_in.wait()
    gain_in.wait()
    floated = tokens[...].astype(jnp.float32)
    mean_square = jnp.mean(floated * floated, axis=-1, keepdims=True)
    normed = floated * lax.rsqrt(mean_square + epsilon) * gain[...]
    for part in range(pieces):
        for fold in range(folds):
            column = (part * folds + fold) * LANES
            spread[part, pl.ds(fold, own, stride=folds), :] = normed[:, column : column + LANES]
    piece[...] = spread[...].astype(jnp.bfloat16)
    for part in range(pieces):
        gathered[core, part, chip] = piece[part]
    pl.semaphore_wait(barrier, chips)

    def announce(part, step):
        pltpu.make_async_remote_copy(
            src_ref=piece.at[part],
            dst_ref=gathered.at[core, part, chip],
            send_sem=ag_send_sem,
            recv_sem=ag_recv_sem.at[part],
            device_id=at(peer(step), core),
            device_id_type=MESH,
        ).start()

    def forward(part):
        return pltpu.make_async_remote_copy(
            src_ref=gathered.at[core, part],
            dst_ref=gathered.at[core, part],
            send_sem=fwd_send_sem.at[part],
            recv_sem=fwd_recv_sem.at[part],
            device_id=at(chip, other),
            device_id_type=MESH,
        )

    def collect(part):
        whole_wait(gathered.at[core, part, pl.ds(0, chips - 1)], ag_recv_sem.at[part])
        forward(part).start()

    def assemble(part):
        forward(part).wait_recv()
        gathered_f32[...] = gathered[:, part].astype(jnp.float32).reshape(gathered_f32.shape)
        for fold in range(folds):
            place = part * folds + fold
            x[place // per_step, :, pl.ds(place % per_step * LANES, LANES)] = gathered_f32[
                pl.ds(fold, rows, stride=folds), :
            ].astype(jnp.bfloat16)

    def project(step):
        slot = step % slots
        for part in range(2):
            weight_copy(step, part).wait()
        for part in range(parts):
            for column in range(0, width, TILE):
                stop = min(column + TILE, width)
                product = jnp.dot(x[step], ring[slot, part, :, column:stop], preferred_element_type=jnp.float32)
                if step == 0:
                    acc[part, :, column:stop] = product
                else:
                    acc[part, :, column:stop] += product
        if step + slots < k_steps:
            for part in range(2):
                weight_copy(step + slots, part).start()
        ahead = step + slots - k_steps
        if 0 <= ahead < down_slots:
            down_copy(ahead).start()

    for part in range(pieces):
        each(1, chips, functools.partial(announce, part))
    collect(0)
    for part in range(pieces):
        assemble(part)
        steps = range(part * k_steps // pieces, (part + 1) * k_steps // pieces)
        for step in steps:
            project(step)
            if step == steps[0] and part + 1 < pieces:
                collect(part + 1)
    for ahead in range(max(0, min(slots, down_slots)), down_slots):
        down_copy(ahead).start()

    if parts == 1:
        gate_out, up_out = acc[0, :, :units], acc[0, :, units:]
    else:
        gate_out, up_out = acc[0], acc[1]
    hidden[...] = (gate_out / (1.0 + jnp.exp(-gate_out)) * up_out).astype(jnp.bfloat16)

    def sibling(part):
        _, _, sib_send, sib_recv, _, _, send_sem, recv_sem, _, _ = groups[part]
        return pltpu.make_async_remote_copy(
            src_ref=sib_send,
            dst_ref=sib_recv,
            send_sem=send_sem,
            recv_sem=recv_sem,
            device_id=at(chip, other),
            device_id_type=MESH,
        )

    def produce(part, first):
        partial, mine, sib_send = groups[part][:3]
        half = mine.shape[0]
        span = partial.shape[0] // rows
        chunks = span * LANES // N_CHUNK
        for chunk in range(chunks):
            step = first + chunk
            down_copy(step).wait()
            for column in range(0, N_CHUNK, TILE):
                product = jnp.dot(
                    hidden[...],
                    down_ring[step % down_slots, :, column : column + TILE],
                    preferred_element_type=jnp.float32,
                )
                for lane in range(0, TILE, LANES):
                    fold = (chunk * N_CHUNK + column + lane) // LANES
                    partial[pl.ds(fold, rows, stride=span), :] = product[:, lane : lane + LANES]
            if step + down_slots < n_steps:
                down_copy(step + down_slots).start()
        sib_send[...] = partial[pl.ds(pl.multiple_of(other * half, half), half), :].astype(jnp.bfloat16)
        mine[...] = partial[pl.ds(pl.multiple_of(core * half, half), half), :]
        sibling(part).start()
        return first + chunks

    def exchange(part):
        _, mine, _, sib_recv, chip_send, chip_recv, _, _, send_sem, recv_sem = groups[part]
        sibling(part).wait_recv()
        both = mine[...] + sib_recv[...].astype(jnp.float32)
        chip_send[...] = both.astype(jnp.bfloat16).reshape(chip_send.shape)

        def send(ahead):
            to = peer(ahead)
            pltpu.make_async_remote_copy(
                src_ref=chip_send.at[to],
                dst_ref=chip_recv.at[chip],
                send_sem=send_sem,
                recv_sem=recv_sem,
                device_id=at(to, core),
                device_id_type=MESH,
            ).start()

        each(1, chips, send)
        chip_recv[chip] = chip_send[chip]

    def finish(part, first):
        mine, chip_recv, recv_sem = groups[part][1], groups[part][5], groups[part][9]
        whole_wait(chip_recv.at[pl.ds(0, chips - 1)], recv_sem)
        count = chip_recv.shape[1]
        mine[pl.ds(0, count), :] = jnp.sum(chip_recv[...].astype(jnp.float32), axis=0)
        span = count // own
        for fold in range(span):
            out_ref[:, pl.ds(first * N_CHUNK + fold * LANES, LANES)] = mine[
                pl.ds(fold, own, stride=span), :
            ].astype(jnp.bfloat16)

    firsts = [0]
    last = len(groups) - 1
    for part in range(last + 1):
        firsts.append(produce(part, firsts[-1]))
        if part >= 1:
            exchange(part - 1)
    for part in range(last - 1):
        finish(part, firsts[part])
    exchange(last)
    for part in range(max(0, last - 1), last + 1):
        finish(part, firsts[part])

    for part in range(last + 1):
        sibling(part).wait_send()
        whole_wait(groups[part][4].at[pl.ds(0, chips - 1)], groups[part][8])
    for part in range(pieces):
        forward(part).wait_send()
        whole_wait(gathered.at[core, part, pl.ds(0, chips - 1)], ag_send_sem)


def per_device(devices, tokens, norm_gain, gate_weight, up_weight, down_weight):
    own, features = tokens.shape
    units = gate_weight.shape[1]
    chips = devices // 2
    rows = devices * own
    folds = features // LANES // PIECES
    k_steps, n_steps = features // K_CHUNK, features // N_CHUNK
    slots, down_slots = min(RING, k_steps), min(DOWN_RING, n_steps)
    parts = 1 if units % LANES == 0 else 2
    width = 2 * units // parts
    bf16, f32 = jnp.bfloat16, jnp.float32
    dma = pltpu.SemaphoreType.DMA
    wide = (n_steps - 2) // WIDE
    chunks = [WIDE] * wide + [1] * (n_steps - WIDE * wide)
    groups = []
    for count in chunks:
        span = count * N_CHUNK // LANES
        half = chips * own * span
        groups += [
            pltpu.VMEM((rows * span, LANES), f32),
            pltpu.VMEM((half, LANES), f32),
            pltpu.VMEM((half, LANES), bf16),
            pltpu.VMEM((half, LANES), bf16),
            pltpu.VMEM((chips, own * span, LANES), bf16),
            pltpu.VMEM((chips, own * span, LANES), bf16),
            dma,
            dma,
            dma,
            dma,
        ]
    return pl.pallas_call(
        functools.partial(kernel, chips),
        out_shape=jax.ShapeDtypeStruct((own, features), bf16),
        in_specs=[pl.BlockSpec(memory_space=pl.ANY)] * 5,
        out_specs=pl.BlockSpec(memory_space=pltpu.VMEM),
        scratch_shapes=[
            pltpu.VMEM((own, features), bf16),
            pltpu.VMEM((1, features), f32),
            pltpu.VMEM((PIECES, own * folds, LANES), f32),
            pltpu.VMEM((PIECES, own * folds, LANES), bf16),
            pltpu.VMEM((2, PIECES, chips, own * folds, LANES), bf16),
            pltpu.VMEM((rows * folds, LANES), f32),
            pltpu.VMEM((k_steps, rows, K_CHUNK), bf16),
            pltpu.VMEM((slots, parts, K_CHUNK, width), bf16),
            pltpu.VMEM((down_slots, units, N_CHUNK), bf16),
            pltpu.VMEM((parts, rows, width), f32),
            pltpu.VMEM((rows, units), bf16),
            dma((2,)),
            dma((slots, 2)),
            dma((down_slots,)),
            dma,
            dma((PIECES,)),
            dma((PIECES,)),
            dma((PIECES,)),
            *groups,
        ],
        compiler_params=pltpu.CompilerParams(
            collective_id=0, has_side_effects=True, vmem_limit_bytes=60 * 1024 * 1024
        ),
        cost_estimate=pl.CostEstimate(
            flops=6 * rows * features * units,
            bytes_accessed=6 * features * units,
            transcendentals=rows * units,
        ),
    )(tokens, norm_gain.reshape(1, features), gate_weight, up_weight, down_weight)


def solution(mesh):
    placed = (P(("groups", "row"), None), P(), P(None, "row"), P(None, "row"), P("row", None))
    return jax.shard_map(
        functools.partial(per_device, mesh.shape["row"]),
        mesh=mesh,
        in_specs=placed,
        out_specs=P(("groups", "row"), None),
        check_vma=False,
    )
```

```python
import functools

import jax
import jax.numpy as jnp
from jax import lax
from jax.experimental import pallas as pl
from jax.experimental.pallas import tpu as pltpu
from jax.sharding import PartitionSpec as P

epsilon = 1e-05
LANES = 128
TILE = 256
K_CHUNK = 1024
N_CHUNK = 2048
RING = 6
DOWN_RING = 4
D_CHUNK = 1024
PIECES = 4
LAG = 3
EARLY = 0
MESH = pl.DeviceIdType.MESH


def whole_wait(ref, sem):
    pltpu.make_async_copy(ref, ref, sem).wait()


def each(start, stop, body):
    pl.loop(start, stop)(body)


def kernel(
    chips,
    tokens_hbm,
    gain_hbm,
    gate_hbm,
    up_hbm,
    down_hbm,
    out_ref,
    tokens,
    gain,
    spread,
    piece,
    gathered,
    gathered_f32,
    x,
    ring,
    down_ring,
    acc,
    hidden,
    in_sem,
    ring_sem,
    down_sem,
    ag_send_sem,
    ag_recv_sem,
    fwd_send_sem,
    fwd_recv_sem,
    partial,
    mine,
    sib_send,
    sib_recv,
    chip_send,
    chip_recv,
    total,
    sib_send_sem,
    sib_recv_sem,
    chip_send_sem,
    chip_recv_sem,
):
    own, features = tokens.shape
    units = gate_hbm.shape[1]
    slots, parts, _, width = ring.shape
    down_slots = down_ring.shape[0]
    k_steps = features // K_CHUNK
    n_steps = features // N_CHUNK
    pieces = spread.shape[0]
    folds = features // LANES // pieces
    per_step = K_CHUNK // LANES
    rows = 2 * chips * own
    per_piece = k_steps // pieces
    fan = max(1, min(2, down_slots))
    subs, d_steps = N_CHUNK // D_CHUNK, features // D_CHUNK
    half, span = mine.shape[1], N_CHUNK // LANES
    group = lax.axis_index("groups")
    me = lax.axis_index("row")
    core = lax.rem(me, 2)
    chip = me // 2
    other = 1 - core

    def at(to_chip, to_core):
        return (group, 2 * to_chip + to_core)

    def peer(step):
        return lax.rem(chip + step, chips)

    barrier = pltpu.get_barrier_semaphore()
    pl.semaphore_signal(barrier, inc=1, device_id=at(chip, other), device_id_type=MESH)
    each(
        1,
        chips,
        lambda step: pl.semaphore_signal(barrier, inc=1, device_id=at(peer(step), core), device_id_type=MESH),
    )
    tokens_in = pltpu.make_async_copy(tokens_hbm, tokens, in_sem.at[0])
    gain_in = pltpu.make_async_copy(gain_hbm, gain, in_sem.at[1])
    tokens_in.start()
    gain_in.start()

    def weight_copy(step, part):
        slot = lax.rem(step, slots)
        if parts == 1:
            to = ring.at[slot, 0, :, pl.ds(part * units, units)]
        else:
            to = ring.at[slot, part]
        return pltpu.make_async_copy(
            (gate_hbm, up_hbm)[part].at[pl.ds(pl.multiple_of(step * K_CHUNK, K_CHUNK), K_CHUNK)],
            to,
            ring_sem.at[slot, part],
        )

    def down_copy(step):
        slot = lax.rem(step, down_slots)
        return pltpu.make_async_copy(
            down_hbm.at[:, pl.ds(pl.multiple_of(step * D_CHUNK, D_CHUNK), D_CHUNK)],
            down_ring.at[slot],
            down_sem.at[slot],
        )

    def fill(step):
        for part in range(2):
            weight_copy(step, part).start()

    each(0, slots, fill)

    tokens_in.wait()
    gain_in.wait()
    floated = tokens[...].astype(jnp.float32)
    mean_square = jnp.mean(floated * floated, axis=-1, keepdims=True)
    normed = floated * lax.rsqrt(mean_square + epsilon) * gain[...]
    for part in range(pieces):
        for fold in range(folds):
            column = (part * folds + fold) * LANES
            spread[part, pl.ds(fold, own, stride=folds), :] = normed[:, column : column + LANES]
    piece[...] = spread[...].astype(jnp.bfloat16)
    for part in range(pieces):
        gathered[core, part, chip] = piece[part]
    pl.semaphore_wait(barrier, chips)

    def announce(part, step):
        pltpu.make_async_remote_copy(
            src_ref=piece.at[part],
            dst_ref=gathered.at[core, part, chip],
            send_sem=ag_send_sem,
            recv_sem=ag_recv_sem.at[part],
            device_id=at(peer(step), core),
            device_id_type=MESH,
        ).start()

    def forward(part):
        return pltpu.make_async_remote_copy(
            src_ref=gathered.at[core, part],
            dst_ref=gathered.at[core, part],
            send_sem=fwd_send_sem.at[part],
            recv_sem=fwd_recv_sem.at[part],
            device_id=at(chip, other),
            device_id_type=MESH,
        )

    def collect(part):
        whole_wait(gathered.at[core, part, pl.ds(0, chips - 1)], ag_recv_sem.at[part])
        forward(part).start()

    def assemble(part):
        forward(part).wait_recv()
        gathered_f32[...] = gathered[:, part].astype(jnp.float32).reshape(gathered_f32.shape)
        for fold in range(folds):
            x[part * per_piece + fold // per_step, :, pl.ds(fold % per_step * LANES, LANES)] = gathered_f32[
                pl.ds(fold, rows, stride=folds), :
            ].astype(jnp.bfloat16)

    def project(step):
        part, within = step // per_piece, lax.rem(step, per_piece)

        @pl.when(within == 0)
        def _():
            assemble(part)

        slot = lax.rem(step, slots)
        for half_of in range(2):
            weight_copy(step, half_of).wait()
        for half_of in range(parts):
            for column in range(0, width, TILE):
                stop = min(column + TILE, width)
                acc[half_of, :, column:stop] += jnp.dot(
                    x[step], ring[slot, half_of, :, column:stop], preferred_element_type=jnp.float32
                )

        @pl.when(step + slots < k_steps)
        def _():
            fill(step + slots)

        ahead = step + slots - k_steps

        @pl.when(jnp.logical_and(ahead >= 0, ahead < down_slots // fan))
        def _():
            for which in range(fan):
                down_copy(ahead * fan + which).start()

        @pl.when(jnp.logical_and(within == 0, part + 1 < pieces))
        def _():
            collect(part + 1)

    @pl.loop(0, pieces)
    def _(part):
        each(1, chips, functools.partial(announce, part))

    acc[...] = jnp.zeros_like(acc)
    collect(0)
    each(0, k_steps, project)
    each(min(slots, down_slots // fan) * fan, down_slots, lambda ahead: down_copy(ahead).start())

    if parts == 1:
        gate_out, up_out = acc[0, :, :units], acc[0, :, units:]
    else:
        gate_out, up_out = acc[0], acc[1]
    hidden[...] = (gate_out / (1.0 + jnp.exp(-gate_out)) * up_out).astype(jnp.bfloat16)

    def sibling(step):
        return pltpu.make_async_remote_copy(
            src_ref=sib_send.at[step],
            dst_ref=sib_recv.at[step],
            send_sem=sib_send_sem.at[step],
            recv_sem=sib_recv_sem.at[step],
            device_id=at(chip, other),
            device_id_type=MESH,
        )

    def produce(step):
        for sub in range(subs):
            chunk = step * subs + sub
            down_copy(chunk).wait()
            slot = lax.rem(chunk, down_slots)
            for column in range(0, D_CHUNK, TILE):
                product = jnp.dot(
                    hidden[...], down_ring[slot, :, column : column + TILE], preferred_element_type=jnp.float32
                )
                for lane in range(0, TILE, LANES):
                    fold = (sub * D_CHUNK + column + lane) // LANES
                    partial[pl.ds(fold, rows, stride=span), :] = product[:, lane : lane + LANES]

            @pl.when(chunk + down_slots < d_steps)
            def _():
                down_copy(chunk + down_slots).start()

            if sub == EARLY:
                pl.when(step >= 1)(lambda: exchange(step - 1))

        sib_send[step] = partial[pl.ds(pl.multiple_of(other * half, half), half), :].astype(jnp.bfloat16)
        mine[step] = partial[pl.ds(pl.multiple_of(core * half, half), half), :]
        sibling(step).start()

    def exchange(step):
        sibling(step).wait_recv()
        both = mine[step] + sib_recv[step].astype(jnp.float32)
        chip_send[step] = both.astype(jnp.bfloat16).reshape(chip_send.shape[1:])

        def send(ahead):
            to = peer(ahead)
            pltpu.make_async_remote_copy(
                src_ref=chip_send.at[step, to],
                dst_ref=chip_recv.at[step, chip],
                send_sem=chip_send_sem.at[step],
                recv_sem=chip_recv_sem.at[step],
                device_id=at(to, core),
                device_id_type=MESH,
            ).start()

        each(1, chips, send)
        chip_recv[step, chip] = chip_send[step, chip]

    def finish(step):
        whole_wait(chip_recv.at[step, pl.ds(0, chips - 1)], chip_recv_sem.at[step])
        total[...] = jnp.sum(chip_recv[step].astype(jnp.float32), axis=0)
        for fold in range(span):
            out_ref[:, pl.ds(pl.multiple_of(step * N_CHUNK, N_CHUNK) + fold * LANES, LANES)] = total[
                pl.ds(fold, own, stride=span), :
            ].astype(jnp.bfloat16)

    @pl.loop(0, n_steps + LAG)
    def _(step):
        pl.when(step < n_steps)(lambda: produce(step))
        pl.when(step == n_steps)(lambda: exchange(step - 1))
        pl.when(step >= LAG)(lambda: finish(step - LAG))

    @pl.loop(0, n_steps)
    def _(step):
        sibling(step).wait_send()
        whole_wait(chip_send.at[step, pl.ds(0, chips - 1)], chip_send_sem.at[step])

    @pl.loop(0, pieces)
    def _(part):
        forward(part).wait_send()
        whole_wait(gathered.at[core, part, pl.ds(0, chips - 1)], ag_send_sem)


def per_device(devices, tokens, norm_gain, gate_weight, up_weight, down_weight):
    own, features = tokens.shape
    units = gate_weight.shape[1]
    chips = devices // 2
    rows = devices * own
    folds = features // LANES // PIECES
    k_steps, n_steps = features // K_CHUNK, features // N_CHUNK
    slots, down_slots = min(RING, k_steps), min(DOWN_RING, features // D_CHUNK)
    parts = 1 if units % LANES == 0 else 2
    width = 2 * units // parts
    bf16, f32 = jnp.bfloat16, jnp.float32
    dma = pltpu.SemaphoreType.DMA
    span = N_CHUNK // LANES
    half = chips * own * span
    return pl.pallas_call(
        functools.partial(kernel, chips),
        out_shape=jax.ShapeDtypeStruct((own, features), bf16),
        in_specs=[pl.BlockSpec(memory_space=pl.ANY)] * 5,
        out_specs=pl.BlockSpec(memory_space=pltpu.VMEM),
        scratch_shapes=[
            pltpu.VMEM((own, features), bf16),
            pltpu.VMEM((1, features), f32),
            pltpu.VMEM((PIECES, own * folds, LANES), f32),
            pltpu.VMEM((PIECES, own * folds, LANES), bf16),
            pltpu.VMEM((2, PIECES, chips, own * folds, LANES), bf16),
            pltpu.VMEM((rows * folds, LANES), f32),
            pltpu.VMEM((k_steps, rows, K_CHUNK), bf16),
            pltpu.VMEM((slots, parts, K_CHUNK, width), bf16),
            pltpu.VMEM((down_slots, units, D_CHUNK), bf16),
            pltpu.VMEM((parts, rows, width), f32),
            pltpu.VMEM((rows, units), bf16),
            dma((2,)),
            dma((slots, 2)),
            dma((down_slots,)),
            dma,
            dma((PIECES,)),
            dma((PIECES,)),
            dma((PIECES,)),
            pltpu.VMEM((rows * span, LANES), f32),
            pltpu.VMEM((n_steps, half, LANES), f32),
            pltpu.VMEM((n_steps, half, LANES), bf16),
            pltpu.VMEM((n_steps, half, LANES), bf16),
            pltpu.VMEM((n_steps, chips, own * span, LANES), bf16),
            pltpu.VMEM((n_steps, chips, own * span, LANES), bf16),
            pltpu.VMEM((own * span, LANES), f32),
            dma((n_steps,)),
            dma((n_steps,)),
            dma((n_steps,)),
            dma((n_steps,)),
        ],
        compiler_params=pltpu.CompilerParams(
            collective_id=0, has_side_effects=True, vmem_limit_bytes=60 * 1024 * 1024
        ),
        cost_estimate=pl.CostEstimate(
            flops=6 * rows * features * units,
            bytes_accessed=6 * features * units,
            transcendentals=rows * units,
        ),
    )(tokens, norm_gain.reshape(1, features), gate_weight, up_weight, down_weight)


def solution(mesh):
    placed = (P(("groups", "row"), None), P(), P(None, "row"), P(None, "row"), P("row", None))
    return jax.shard_map(
        functools.partial(per_device, mesh.shape["row"]),
        mesh=mesh,
        in_specs=placed,
        out_specs=P(("groups", "row"), None),
        check_vma=False,
    )
```
